32 devices in a mesh: groups: 2 (over x), dp: 16 (over z, y, core).
Axes of the slice: x: 2, y: 2, z: 4, core: 2. Of those that a mesh axis runs over, the one named last changes fastest.
Arguments:
- queries: bfloat16 [256, 4096], P(('groups', 'dp')), parts along dimension 0, may hold values from -0.4 to 0.4
- passages: bfloat16 [256, 4096], P(('groups', 'dp')), parts along dimension 0, may hold values from -0.6 to 0.6
- negatives: bfloat16 [8192, 4096], P(('groups', 'dp')), parts along dimension 0, may hold values from -0.5 to 0.5
- pairs: int32 [3584, 2], P(('groups', 'dp')), parts along dimension 0, may hold values from 0 to 4095, as said below
Outputs:
- losses: float32 [256], P(('groups', 'dp')), parts along dimension 0
- grad_queries: float32 [256, 4096], P(('groups', 'dp')), parts along dimension 0
- grad_passages: float32 [256, 4096], P(('groups', 'dp')), parts along dimension 0
- grad_negatives: float32 [8192, 4096], P(('groups', 'dp')), parts along dimension 0
The draws below stay inside these ranges and needn't reach their ends.
There are 2 independent parts, one for each index of `groups`. The reference program is written for one: setup_inputs(seed, part) draws one part's arguments, and reference() takes and returns one part's arrays. A program takes and returns all parts, laid end to end along the dimension named above; each array names one. Nothing has to cross between parts.
Inputs may be any that keep to these rules, and one draw needn't show every extreme that they name: Column 0 is a query of the device holding the pair, below 8; column 1 is a row of negatives. Queries have varying numbers of pairs. Among the 112 pairs of one device at most 7 name rows held by any one device, and in every draw one device holds rows named by exactly 7 pairs of every device.
All inputs are finite; a program needn't handle non-finite values.
Results may differ from the reference program's by a relative error of at most 0.0081.
Values may be sent and summed in bfloat16 or wider, within the bound.
A program may use at most 128 MiB of HBM per device.

```python
import jax
import jax.numpy as jnp
from jax import lax

D = 4096
QD = 8
POOL_DEV = 256
PAIRS = 112
CAP = 7
NQ = 128
POOL = 4096
NPAIRS = 1792
N_DP = 16


def base_rows(key):
    return 0.015625 * jax.random.truncated_normal(jax.random.fold_in(key, 101), -6.0, 6.0, (NQ, D), jnp.float32)


def pair_table(key):
    key = jax.random.fold_in(key, 202)
    first_key, rest_key = jax.random.split(key)
    full_owner = jax.random.randint(first_key, (), 0, N_DP)

    def one_device(device_key):
        key_one, key_two, key_three, key_four = jax.random.split(device_key, 4)
        others = jax.random.permutation(key_one, CAP * N_DP - CAP).astype(jnp.int32)
        others = jnp.where(others >= full_owner * CAP, others + CAP, others)
        slot_list = jnp.concatenate([full_owner * CAP + jnp.arange(CAP, dtype=jnp.int32), others])[:PAIRS]
        owners = (slot_list // CAP)[jax.random.permutation(key_two, PAIRS)]
        row_pick = jax.random.randint(key_three, (PAIRS,), 0, POOL_DEV)
        query_pick = jax.random.randint(key_four, (PAIRS,), 0, QD)
        return jnp.stack([query_pick, owners * POOL_DEV + row_pick], axis=1)
    table = jax.vmap(one_device)(jax.random.split(rest_key, N_DP))
    return table.reshape(NPAIRS, 2).astype(jnp.int32)


def row_factor(key, count, lower, upper):
    return jnp.exp(jax.random.uniform(key, (count, 1), jnp.float32, jnp.log(lower), jnp.log(upper)))


def noise_rows(key, count, width_limit):
    return 0.015625 * jax.random.truncated_normal(key, -width_limit, width_limit, (count, D), jnp.float32)


def draw_queries(key, part):
    base = base_rows(key)
    key = jax.random.fold_in(key, 1)
    factor = row_factor(key, NQ, 0.5, 2.0)
    return (base * factor).astype(jnp.bfloat16)


def draw_passages(key, part):
    base = base_rows(key)
    key = jax.random.fold_in(key, 2)
    key_one, key_two, key_three = jax.random.split(key, 3)
    partner = jax.random.permutation(key_one, NQ)
    noise = noise_rows(key_two, NQ, 6.0)
    factor = row_factor(key_three, NQ, 0.5, 2.0)
    mixed = 0.3 * base + 0.3 * jnp.take(base, partner, axis=0) + 0.9 * noise
    return (mixed * factor).astype(jnp.bfloat16)


def draw_negatives(key, part):
    base = base_rows(key)
    table = pair_table(key)
    key = jax.random.fold_in(key, 3)
    key_two, key_three = jax.random.split(key)
    asker = jnp.arange(NPAIRS, dtype=jnp.int32) // PAIRS * QD + table[:, 0]
    miner = jnp.full((POOL,), -1, jnp.int32).at[table[:, 1]].max(asker)
    picked = jnp.take(base, jnp.maximum(miner, 0), axis=0) * (miner >= 0).astype(jnp.float32)[:, None]
    noise = noise_rows(key_two, POOL, 6.0)
    factor = row_factor(key_three, POOL, 0.5, 2.0)
    return ((0.3 * picked + 0.9 * noise) * factor).astype(jnp.bfloat16)


def draw_pairs(key, part):
    table = pair_table(key)
    return table


def setup_inputs(seed: int = 0, part: int = 0) -> dict:
    arg_keys = jax.random.split(jax.random.key(seed), 5)
    part_splits = jax.random.split(jax.random.fold_in(arg_keys[4], part), 5)
    return {
        "queries": draw_queries(jax.random.fold_in(jax.random.fold_in(arg_keys[4], part), 71), part),
        "passages": draw_passages(jax.random.fold_in(jax.random.fold_in(arg_keys[4], part), 71), part),
        "negatives": draw_negatives(jax.random.fold_in(jax.random.fold_in(arg_keys[4], part), 71), part),
        "pairs": draw_pairs(jax.random.fold_in(jax.random.fold_in(arg_keys[4], part), 71), part),
    }


inv_temp = 50.0
norm_eps = 1e-06

def unit_rows(source_rows):
    raw_values = source_rows.astype(jnp.float32)
    row_scale = lax.rsqrt(lax.optimization_barrier(jnp.sum(raw_values * raw_values, axis=1, keepdims=True)) + norm_eps)
    return (raw_values, row_scale, (raw_values * row_scale).astype(jnp.bfloat16))

def norm_grad(raw_values, row_scale, upstream):
    dot_sum = lax.optimization_barrier(jnp.sum(raw_values * upstream, axis=1, keepdims=True))
    return row_scale * upstream - row_scale * row_scale * row_scale * dot_sum * raw_values

def reference(queries, passages, negatives, pairs):
    query_vals, query_scale, query_unit = unit_rows(queries)
    passage_vals, passage_scale, passage_unit = unit_rows(passages)
    negative_vals, negative_scale, negative_unit = unit_rows(negatives)
    holder = (jnp.arange(NPAIRS) // PAIRS).astype(jnp.int32)
    query_of = (holder * QD + pairs[:, 0]).astype(jnp.int32)
    target = pairs[:, 1].astype(jnp.int32)
    hard_rows = jnp.take(negative_unit, target, axis=0)
    asking = jnp.take(query_unit, query_of, axis=0)
    hard_score = inv_temp * lax.optimization_barrier(jnp.sum(asking.astype(jnp.float32) * hard_rows.astype(jnp.float32), axis=1))
    scores = inv_temp * jnp.dot(query_unit, passage_unit.T, preferred_element_type=jnp.float32)
    hard_sums = jax.ops.segment_sum(jnp.exp(hard_score), query_of, num_segments=NQ)
    log_total = jnp.log(lax.optimization_barrier(jnp.sum(jnp.exp(scores), axis=1)) + hard_sums)
    losses = log_total - jnp.diagonal(scores)
    identity_matrix = jnp.eye(NQ, dtype=jnp.float32)
    weight = (jnp.exp(scores - log_total[:, None]) - identity_matrix).astype(jnp.bfloat16)
    hard_weight = jnp.exp(hard_score - jnp.take(log_total, query_of)).astype(jnp.bfloat16)
    hard_terms = hard_weight.astype(jnp.float32)[:, None] * hard_rows.astype(jnp.float32)
    query_grad = inv_temp * (jnp.dot(weight, passage_unit, preferred_element_type=jnp.float32) + jax.ops.segment_sum(hard_terms, query_of, num_segments=NQ))
    passage_grad = inv_temp * jnp.dot(weight.T, query_unit, preferred_element_type=jnp.float32)
    pool_terms = hard_weight.astype(jnp.float32)[:, None] * asking.astype(jnp.float32)
    pool_grad = inv_temp * jax.ops.segment_sum(pool_terms, target, num_segments=POOL)
    return (losses, norm_grad(query_vals, query_scale, query_grad), norm_grad(passage_vals, passage_scale, passage_grad), norm_grad(negative_vals, negative_scale, pool_grad))
```

```python
import functools

import jax
import jax.numpy as jnp
from jax import lax
from jax.experimental import pallas as pl
from jax.experimental.pallas import tpu as pltpu
from jax.sharding import PartitionSpec as P

inv_temp = 50.0
norm_eps = 1e-06
f32 = jnp.float32
bf16 = jnp.bfloat16
EXTRA = 128


def dot_nt(a, b):
    return lax.dot_general(a, b, (((1,), (1,)), ((), ())), preferred_element_type=f32)


def dot_nn(a, b):
    return lax.dot_general(a, b, (((1,), (0,)), ((), ())), preferred_element_type=f32)


def norm_grad(raw, scale, up):
    dot_sum = jnp.sum(raw * up, axis=1, keepdims=True)
    return scale * up - scale * scale * scale * dot_sum * raw


def kernel(
    n, q_ref, p_ref, neg_ref, pairs_ref,
    loss_ref, gq_ref, gp_ref, gn_ref,
    qbuf, qfull, nraw, unit, nscale, counts, scores, expt, weights, ubuf, sibrecv, crecv, gnbuf,
    zsend, zsib, zbuf, acc,
    nsem, gsem, qs, qr, fs, fr, us, ur, cs, cr, zs, zr, zxs, zxr,
):
    qd, width = q_ref.shape
    half = width // 2
    pool = neg_ref.shape[0]
    npairs = pairs_ref.shape[0]
    nq = n * qd
    nc = n // 2
    me = lax.axis_index("dp")
    chip = me // 2
    core = me - 2 * chip
    sib = me + 1 - 2 * core

    def ahead(k):
        return lax.rem(chip + k, nc)

    def behind(k):
        return lax.rem(chip + nc - k, nc)

    def remote(src, dst, ssem, rsem, target):
        return pltpu.make_async_remote_copy(
            src_ref=src, dst_ref=dst, send_sem=ssem, recv_sem=rsem,
            device_id={"dp": target}, device_id_type=pl.DeviceIdType.MESH,
        )

    load = pltpu.make_async_copy(neg_ref, nraw, nsem)
    load.start()
    barrier = pltpu.get_barrier_semaphore()
    pl.semaphore_signal(barrier, inc=1, device_id={"dp": sib}, device_id_type=pl.DeviceIdType.MESH)

    @pl.loop(1, nc)
    def _(k):
        pl.semaphore_signal(
            barrier, inc=1, device_id={"dp": 2 * ahead(k) + core},
            device_id_type=pl.DeviceIdType.MESH,
        )

    qx = q_ref[...].astype(f32)
    qscale = lax.rsqrt(jnp.sum(qx * qx, axis=1, keepdims=True) + norm_eps)
    qu = qx * qscale
    qbuf[me, :, :half] = jnp.concatenate([qu[:, :half], qu[:, half:]], axis=0).astype(bf16)
    pv = pairs_ref[...].astype(f32)
    diag = lax.broadcasted_iota(jnp.int32, (npairs, EXTRA), 0) == lax.broadcasted_iota(
        jnp.int32, (npairs, EXTRA), 1
    )
    prow = jnp.sum(jnp.where(diag, pv[:, 0:1], 0.0), axis=0, keepdims=True)
    trow = jnp.sum(jnp.where(diag, pv[:, 1:2], 0.0), axis=0, keepdims=True)
    owner = jnp.floor((trow + 0.5) * (1.0 / pool))
    local_row = trow - owner * pool
    owner = jnp.where(lax.broadcasted_iota(jnp.int32, (1, EXTRA), 1) < npairs, owner, -1.0)
    rid = lax.broadcasted_iota(jnp.int32, (16, EXTRA), 0)
    meta = jnp.where(rid == 0, prow, jnp.where(rid == 1, owner, local_row))
    qbuf[me, :, half:] = meta.astype(bf16)

    pl.semaphore_wait(barrier, nc)

    def q_copy(k, target):
        return remote(qbuf.at[me], qbuf.at[me], qs.at[k], qr.at[k], target)

    @pl.loop(1, nc)
    def _(k):
        q_copy(k, 2 * ahead(k) + core).start()

    q_copy(0, sib).start()

    px = p_ref[...].astype(f32)
    pscale = lax.rsqrt(jnp.sum(px * px, axis=1, keepdims=True) + norm_eps)
    unit[pool : pool + 16, :] = jnp.concatenate(
        [px * pscale, jnp.zeros((16 - qd, width), f32)], axis=0
    ).astype(bf16)
    unit[pool + 16 :, :] = jnp.zeros((unit.shape[0] - pool - 16, width), bf16)
    load.wait()

    @pl.loop(0, pool // 16)
    def _(b):
        rows = pl.ds(pl.multiple_of(b * 16, 16), 16)
        x = nraw[rows, :].astype(f32)
        s = lax.rsqrt(jnp.sum(x * x, axis=1, keepdims=True) + norm_eps)
        nscale[rows, :] = s
        unit[rows, :] = (x * s).astype(bf16)

    def f_copy(k, c):
        slot = 2 * behind(k) + c
        return remote(qbuf.at[slot], qbuf.at[slot], fs.at[k], fr.at[k], sib)

    @pl.loop(1, nc)
    def _(k):
        slot = 2 * behind(k) + core
        remote(qbuf.at[slot], qbuf.at[slot], qs.at[k], qr.at[k], sib).wait_recv()
        f_copy(k, core).start()

    arow = lax.broadcasted_iota(jnp.int32, (unit.shape[0], nq), 0)
    counts[...] = jnp.where((arow >= pool) & (arow < pool + qd), 1.0, 0.0)
    mef = me.astype(f32)

    def place(j):
        a = qbuf[2 * j].astype(f32)
        b = qbuf[2 * j + 1].astype(f32)
        rows = pl.ds(pl.multiple_of(j * 16, 16), 16)
        qfull[rows, :half] = jnp.concatenate([a[:8, :half], b[:8, :half]], axis=0).astype(bf16)
        qfull[rows, half:] = jnp.concatenate([a[8:, :half], b[8:, :half]], axis=0).astype(bf16)
        pool_id = lax.broadcasted_iota(jnp.int32, (pool, EXTRA), 0).astype(f32)
        query_id = lax.broadcasted_iota(jnp.int32, (nq, EXTRA), 0).astype(f32)
        hot_t, hot_q = [], []
        for part, c in ((a, 0), (b, 1)):
            m = part[:8, half:]
            want = jnp.where(m[1:2] == mef, m[2:3], -1.0)
            ask = m[0:1] + ((2 * j + c) * qd).astype(f32)
            hot_t.append(jnp.where(pool_id == want, 1.0, 0.0).astype(bf16))
            hot_q.append(jnp.where(query_id == ask, 1.0, 0.0).astype(bf16))
        counts[:pool, :] += dot_nt(
            jnp.concatenate(hot_t, axis=1), jnp.concatenate(hot_q, axis=1)
        )

    remote(qbuf.at[sib], qbuf.at[sib], qs.at[0], qr.at[0], sib).wait_recv()
    place(chip)

    @pl.loop(1, nc)
    def _(k):
        f_copy(k, 1 - core).wait_recv()
        place(behind(k))

    zero = jnp.zeros((1, 128), f32)
    for m in range(nq // 128):
        cols = slice(m * 128, m * 128 + 128)
        s = inv_temp * dot_nt(unit[...], qfull[cols, :])
        scores[:, cols] = s
        e = counts[:, cols] * jnp.exp(s)
        zsend[:, cols] = jnp.broadcast_to(jnp.sum(e, axis=0, keepdims=True) + zero, (8, 128))
        expt[cols, :] = e.T.astype(bf16)

    z_sib = remote(zsend, zsib, zs.at[0], zr.at[0], sib)
    z_sib.start()

    step = 256

    @pl.loop(0, half // step)
    def _(b):
        left = pl.ds(pl.multiple_of(b * step, step), step)
        right = pl.ds(pl.multiple_of(half + b * step, step), step)
        for m in range(nq // 128):
            e = expt[m * 128 : m * 128 + 128, :]
            u0 = dot_nn(e, unit[:, left]).reshape(128 // 8, 8, step)
            u1 = dot_nn(e, unit[:, right]).reshape(128 // 8, 8, step)
            ubuf[m * 16 : m * 16 + 16, :, left] = jnp.concatenate([u0, u1], axis=1).astype(bf16)

    def u_copy(k, j):
        return remote(ubuf.at[2 * j + 1 - core], sibrecv.at[j], us.at[k], ur.at[k], sib)

    @pl.loop(1, nc + 1)
    def _(k):
        u_copy(lax.rem(k, nc), ahead(k)).start()

    z_sib.wait_recv()
    zbuf[chip] = zsend[...] + zsib[...]

    def z_copy(k, slot):
        return remote(zbuf.at[chip], zbuf.at[slot], zxs.at[k], zxr.at[k], 2 * ahead(k) + core)

    @pl.loop(1, nc)
    def _(k):
        z_copy(k, chip).start()

    def c_copy(k, j):
        return remote(
            ubuf.at[2 * j + core], crecv.at[k], cs.at[k], cr.at[k], 2 * j + core
        )

    @pl.loop(1, nc)
    def _(k):
        j = ahead(k)
        u_copy(k, j).wait_recv()
        ubuf[2 * j + core] = (
            ubuf[2 * j + core].astype(f32) + sibrecv[j].astype(f32)
        ).astype(bf16)
        c_copy(k, j).start()

    @pl.loop(1, nc)
    def _(k):
        z_copy(k, behind(k)).wait_recv()

    total = zbuf[0]
    for j in range(1, nc):
        total = total + zbuf[j]
    log_total = jnp.log(total)
    lane_q = lax.broadcasted_iota(jnp.int32, (8, nq), 1)
    row_q = lax.broadcasted_iota(jnp.int32, (8, nq), 0)
    own = lane_q == row_q + me * qd
    log_own = jnp.sum(jnp.where(own, log_total, 0.0), axis=1, keepdims=True)
    self_score = jnp.sum(
        jnp.where(own, scores[pool : pool + 8, :], 0.0), axis=1, keepdims=True
    )
    loss_ref[...] = log_own - self_score
    positive = (arow >= pool) & (
        arow - pool + me * qd == lax.broadcasted_iota(jnp.int32, arow.shape, 1)
    ) & (arow < pool + qd)
    w = counts[...] * jnp.exp(scores[...] - log_total[0:1]) - jnp.where(positive, 1.0, 0.0)
    weights[...] = w.astype(bf16)
    udot = jnp.sum(
        weights[:pool, :].astype(f32) * scores[:pool, :], axis=1, keepdims=True
    )

    scale_col = nscale[...]
    back = udot * scale_col
    wide = 512

    @pl.loop(0, width // wide)
    def _(b):
        cols = pl.ds(pl.multiple_of(b * wide, wide), wide)
        g = inv_temp * dot_nn(weights[:pool, :], qfull[:, cols])
        gnbuf[:, cols] = (
            scale_col * (g - back * nraw[:, cols].astype(f32))
        ).astype(bf16)

    save = pltpu.make_async_copy(gnbuf, gn_ref, gsem)
    save.start()

    pg = inv_temp * dot_nn(weights[pool : pool + 16, :], qfull[...])
    gp_ref[...] = norm_grad(px, pscale, pg[:qd])

    own16 = jnp.concatenate([own.astype(f32), jnp.zeros((8, nq), f32)], axis=0).astype(bf16)
    own_w = dot_nt(own16, weights[...]).astype(bf16)
    own_g = dot_nn(own_w, unit[...])[:qd]

    u_copy(0, chip).wait_recv()
    acc[...] = sibrecv[chip].astype(f32)

    @pl.loop(1, nc)
    def _(k):
        c_copy(k, behind(k)).wait_recv()
        acc[...] += crecv[k].astype(f32)

    rest = jnp.concatenate([acc[:8, :], acc[8:, :]], axis=1)
    qg = inv_temp * (own_g + rest * jnp.exp(-log_own))
    gq_ref[...] = norm_grad(qx, qscale, qg)

    q_copy(0, sib).wait_send()
    z_sib.wait_send()
    u_copy(0, chip).wait_send()

    @pl.loop(1, nc)
    def _(k):
        q_copy(k, sib).wait_send()
        f_copy(k, core).wait_send()
        z_copy(k, chip).wait_send()
        u_copy(k, ahead(k)).wait_send()
        c_copy(k, ahead(k)).wait_send()

    save.wait()


def local(queries, passages, negatives, pairs):
    n = lax.axis_size("dp")
    nc = n // 2
    qd, width = queries.shape
    pool = negatives.shape[0]
    nq = n * qd
    half = width // 2
    rows = pool + 128
    vm = pl.BlockSpec(memory_space=pltpu.VMEM)
    anys = pl.BlockSpec(memory_space=pl.ANY)
    dma = pltpu.SemaphoreType.DMA
    loss, gq, gp, gn = pl.pallas_call(
        functools.partial(kernel, n),
        out_shape=(
            jax.ShapeDtypeStruct((qd, 1), f32),
            jax.ShapeDtypeStruct((qd, width), f32),
            jax.ShapeDtypeStruct((qd, width), f32),
            jax.ShapeDtypeStruct((pool, width), bf16),
        ),
        in_specs=[vm, vm, anys, vm],
        out_specs=(vm, vm, vm, anys),
        scratch_shapes=[
            pltpu.VMEM((n, 16, half + EXTRA), bf16),
            pltpu.VMEM((nq, width), bf16),
            pltpu.VMEM((pool, width), bf16),
            pltpu.VMEM((rows, width), bf16),
            pltpu.VMEM((pool, 1), f32),
            pltpu.VMEM((rows, nq), f32),
            pltpu.VMEM((rows, nq), f32),
            pltpu.VMEM((nq, rows), bf16),
            pltpu.VMEM((rows, nq), bf16),
            pltpu.VMEM((n, 16, half), bf16),
            pltpu.VMEM((nc, 16, half), bf16),
            pltpu.VMEM((nc, 16, half), bf16),
            pltpu.VMEM((pool, width), bf16),
            pltpu.VMEM((8, nq), f32),
            pltpu.VMEM((8, nq), f32),
            pltpu.VMEM((nc, 8, nq), f32),
            pltpu.VMEM((16, half), f32),
            dma, dma,
            dma((nc,)), dma((nc,)), dma((nc,)), dma((nc,)), dma((nc,)), dma((nc,)),
            dma((nc,)), dma((nc,)), dma((1,)), dma((1,)), dma((nc,)), dma((nc,)),
        ],
        compiler_params=pltpu.CompilerParams(
            collective_id=0, has_side_effects=True,
            vmem_limit_bytes=(56 if n > 32 else 40) * 1024 * 1024,
        ),
    )(queries, passages, negatives, pairs)
    return loss.reshape(qd), gq, gp, gn.astype(f32)


def solution(mesh):
    rows = P(("groups", "dp"), None)
    return jax.shard_map(
        local,
        mesh=mesh,
        in_specs=(rows, rows, rows, rows),
        out_specs=(P(("groups", "dp")), rows, rows, rows),
        check_vma=False,
    )
```

```python
import functools

import jax
import jax.numpy as jnp
from jax import lax
from jax.experimental import pallas as pl
from jax.experimental.pallas import tpu as pltpu
from jax.sharding import PartitionSpec as P

inv_temp = 50.0
norm_eps = 1e-06
f32 = jnp.float32
bf16 = jnp.bfloat16
EXTRA = 128


def dot_nt(a, b):
    return lax.dot_general(a, b, (((1,), (1,)), ((), ())), preferred_element_type=f32)


def dot_nn(a, b):
    return lax.dot_general(a, b, (((1,), (0,)), ((), ())), preferred_element_type=f32)


def norm_grad(raw, scale, up):
    dot_sum = jnp.sum(raw * up, axis=1, keepdims=True)
    return scale * up - scale * scale * scale * dot_sum * raw


def inner_size(chips):
    size = 1
    while (2 * size) * (2 * size) <= chips and chips % (2 * size) == 0:
        size *= 2
    return size


def kernel(
    n, q_hbm, p_hbm, neg_ref, pairs_hbm,
    loss_ref, gq_ref, gp_ref, gn_ref,
    q_ref, p_ref, pairs_ref, qbuf, qfull, nraw, unit, nscale, counts, scores, expt, weights, ubuf, sibrecv, crecv, gnbuf,
    zsend, zsib, zbuf, acc,
    nsem, insem, gsem, qs, ys, qr, fs, fr, us, ur, cs, cr, zs, zr, zxs, zxr,
):
    qd, width = q_ref.shape
    half = width // 2
    pool = neg_ref.shape[0]
    npairs = pairs_ref.shape[1]
    nq = n * qd
    nc = n // 2
    inner = inner_size(nc)
    outer = nc // inner
    me = lax.axis_index("dp")
    chip = me // 2
    core = me - 2 * chip
    sib = me + 1 - 2 * core

    a = chip // inner
    b = chip - a * inner

    def ahead(k):
        return lax.rem(chip + k, nc)

    def behind(k):
        return lax.rem(chip + nc - k, nc)

    def remote(src, dst, ssem, rsem, target):
        return pltpu.make_async_remote_copy(
            src_ref=src, dst_ref=dst, send_sem=ssem, recv_sem=rsem,
            device_id={"dp": target}, device_id_type=pl.DeviceIdType.MESH,
        )

    first = pltpu.make_async_copy(q_hbm, q_ref, insem.at[0])
    second = pltpu.make_async_copy(pairs_hbm, pairs_ref, insem.at[1])
    third = pltpu.make_async_copy(p_hbm, p_ref, insem.at[2])
    load = pltpu.make_async_copy(neg_ref, nraw, nsem)
    first.start()
    second.start()
    third.start()
    load.start()
    barrier = pltpu.get_barrier_semaphore()
    pl.semaphore_signal(barrier, inc=1, device_id={"dp": sib}, device_id_type=pl.DeviceIdType.MESH)

    @pl.loop(1, nc)
    def _(k):
        pl.semaphore_signal(
            barrier, inc=1, device_id={"dp": 2 * ahead(k) + core},
            device_id_type=pl.DeviceIdType.MESH,
        )

    first.wait()
    qx = q_ref[...].astype(f32)
    qscale = lax.rsqrt(jnp.sum(qx * qx, axis=1, keepdims=True) + norm_eps)
    qu = qx * qscale
    qbuf[me, :, :half] = jnp.concatenate([qu[:, :half], qu[:, half:]], axis=0).astype(bf16)
    second.wait()
    pv = jnp.concatenate(
        [pairs_ref[...].astype(f32), jnp.full((2, EXTRA - npairs), -1.0, f32)], axis=1
    )
    prow, trow = pv[0:1], pv[1:2]
    owner = jnp.floor((trow + 0.5) * (1.0 / pool))
    local_row = trow - owner * pool
    rid = lax.broadcasted_iota(jnp.int32, (16, EXTRA), 0)
    meta = jnp.where(rid == 0, prow, jnp.where(rid == 1, owner, local_row))
    qbuf[me, :, half:] = meta.astype(bf16)

    pl.semaphore_wait(barrier, nc)

    def hop(o, way):
        slot = qbuf.at[2 * o + core]
        target = 2 * (chip + (inner if way == 0 else -inner)) + core
        return remote(slot, slot, qs.at[o, way], qr.at[o], target)

    def across(o, shift):
        slot = qbuf.at[2 * o + core]
        target = 2 * (a * inner + lax.rem(b + shift, inner)) + core
        return remote(slot, slot, ys.at[o, shift], qr.at[o], target)

    def hand(o, c):
        slot = qbuf.at[2 * o + c]
        return remote(slot, slot, fs.at[o], fr.at[o], sib)

    def arrived(o):
        slot = qbuf.at[2 * o + core]
        remote(slot, slot, qs.at[o, 0], qr.at[o], sib).wait_recv()

    def relay(dist, act):
        def column(o, up, down):
            if up is not None:
                @pl.when(up)
                def _():
                    act(hop(o, 0))
            if down is not None:
                @pl.when(down)
                def _():
                    act(hop(o, 1))

            @pl.loop(1, inner)
            def _(shift):
                act(across(o, shift))

            act(hand(o, core))

        if dist == 0:
            column(chip, a + 1 < outer, a > 0)
            return

        @pl.when(a >= dist)
        def _():
            o = chip - dist * inner
            if act is launch:
                arrived(o)
            column(o, a + 1 < outer, None)

        @pl.when(a + dist < outer)
        def _():
            o = chip + dist * inner
            if act is launch:
                arrived(o)
            column(o, None, a > 0)

    def relay_side(dist, act):
        def row(line):
            @pl.loop(1, inner)
            def _(shift):
                o = line * inner + lax.rem(b + inner - shift, inner)
                if act is launch:
                    arrived(o)
                act(hand(o, core))

        if dist == 0:
            row(a)
            return

        @pl.when(a >= dist)
        def _():
            row(a - dist)

        @pl.when(a + dist < outer)
        def _():
            row(a + dist)

    def launch(copy):
        copy.start()

    def sent(copy):
        copy.wait_send()

    relay(0, launch)

    third.wait()
    px = p_ref[...].astype(f32)
    pscale = lax.rsqrt(jnp.sum(px * px, axis=1, keepdims=True) + norm_eps)
    unit[pool : pool + 16, :] = jnp.concatenate(
        [px * pscale, jnp.zeros((16 - qd, width), f32)], axis=0
    ).astype(bf16)
    unit[pool + 16 :, :] = jnp.zeros((unit.shape[0] - pool - 16, width), bf16)
    load.wait()

    def normalise(lo, hi):
        @pl.loop(lo, hi)
        def _(blk):
            rows = pl.ds(pl.multiple_of(blk * 16, 16), 16)
            x = nraw[rows, :].astype(f32)
            s = lax.rsqrt(jnp.sum(x * x, axis=1, keepdims=True) + norm_eps)
            nscale[rows, :] = s
            unit[rows, :] = (x * s).astype(bf16)

    blocks = pool // 16
    normalise(0, blocks // outer)
    for dist in range(1, outer):
        relay(dist, launch)
        relay_side(dist - 1, launch)
        normalise(blocks * dist // outer, blocks * (dist + 1) // outer)
    relay_side(outer - 1, launch)

    arow = lax.broadcasted_iota(jnp.int32, (unit.shape[0], nq), 0)
    counts[...] = jnp.where((arow >= pool) & (arow < pool + qd), 1.0, 0.0)
    mef = me.astype(f32)

    def place(j):
        left = qbuf[2 * j].astype(f32)
        right = qbuf[2 * j + 1].astype(f32)
        rows = pl.ds(pl.multiple_of(j * 16, 16), 16)
        qfull[rows, :half] = jnp.concatenate([left[:8, :half], right[:8, :half]], axis=0).astype(bf16)
        qfull[rows, half:] = jnp.concatenate([left[8:, :half], right[8:, :half]], axis=0).astype(bf16)
        pool_id = lax.broadcasted_iota(jnp.int32, (pool, EXTRA), 0).astype(f32)
        query_id = lax.broadcasted_iota(jnp.int32, (nq, EXTRA), 0).astype(f32)
        hot_t, hot_q = [], []
        for part, c in ((left, 0), (right, 1)):
            m = part[:8, half:]
            want = jnp.where(m[1:2] == mef, m[2:3], -1.0)
            ask = m[0:1] + ((2 * j + c) * qd).astype(f32)
            hot_t.append(jnp.where(pool_id == want, 1.0, 0.0).astype(bf16))
            hot_q.append(jnp.where(query_id == ask, 1.0, 0.0).astype(bf16))
        counts[:pool, :] += dot_nt(
            jnp.concatenate(hot_t, axis=1), jnp.concatenate(hot_q, axis=1)
        )

    hand(chip, 1 - core).wait_recv()
    place(chip)

    @pl.loop(1, nc)
    def _(k):
        hand(behind(k), 1 - core).wait_recv()
        place(behind(k))

    zero = jnp.zeros((1, 128), f32)
    for m in range(nq // 128):
        cols = slice(m * 128, m * 128 + 128)
        s = inv_temp * dot_nt(unit[...], qfull[cols, :])
        scores[:, cols] = s
        e = counts[:, cols] * jnp.exp(s)
        zsend[:, cols] = jnp.broadcast_to(jnp.sum(e, axis=0, keepdims=True) + zero, (8, 128))
        expt[cols, :] = e.T.astype(bf16)

    z_sib = remote(zsend, zsib, zs.at[0], zr.at[0], sib)
    z_sib.start()

    step = 256

    @pl.loop(0, half // step)
    def _(b):
        left = pl.ds(pl.multiple_of(b * step, step), step)
        right = pl.ds(pl.multiple_of(half + b * step, step), step)
        for m in range(nq // 128):
            e = expt[m * 128 : m * 128 + 128, :]
            u0 = dot_nn(e, unit[:, left]).reshape(128 // 8, 8, step)
            u1 = dot_nn(e, unit[:, right]).reshape(128 // 8, 8, step)
            ubuf[m * 16 : m * 16 + 16, :, left] = jnp.concatenate([u0, u1], axis=1).astype(bf16)

    def u_copy(k, j):
        return remote(ubuf.at[2 * j + 1 - core], sibrecv.at[j], us.at[k], ur.at[k], sib)

    @pl.loop(1, nc + 1)
    def _(k):
        u_copy(lax.rem(k, nc), ahead(k)).start()

    z_sib.wait_recv()
    zbuf[chip] = zsend[...] + zsib[...]

    def z_copy(k, slot):
        return remote(zbuf.at[chip], zbuf.at[slot], zxs.at[k], zxr.at[k], 2 * ahead(k) + core)

    @pl.loop(1, nc)
    def _(k):
        z_copy(k, chip).start()

    def c_copy(k, j):
        return remote(
            ubuf.at[2 * j + core], crecv.at[k], cs.at[k], cr.at[k], 2 * j + core
        )

    @pl.loop(1, nc)
    def _(k):
        j = ahead(k)
        u_copy(k, j).wait_recv()
        ubuf[2 * j + core] = (
            ubuf[2 * j + core].astype(f32) + sibrecv[j].astype(f32)
        ).astype(bf16)
        c_copy(k, j).start()

    @pl.loop(1, nc)
    def _(k):
        z_copy(k, behind(k)).wait_recv()

    total = zbuf[0]
    for j in range(1, nc):
        total = total + zbuf[j]
    log_total = jnp.log(total)
    lane_q = lax.broadcasted_iota(jnp.int32, (8, nq), 1)
    row_q = lax.broadcasted_iota(jnp.int32, (8, nq), 0)
    own = lane_q == row_q + me * qd
    log_own = jnp.sum(jnp.where(own, log_total, 0.0), axis=1, keepdims=True)
    self_score = jnp.sum(
        jnp.where(own, scores[pool : pool + 8, :], 0.0), axis=1, keepdims=True
    )
    loss_ref[...] = log_own - self_score
    positive = (arow >= pool) & (
        arow - pool + me * qd == lax.broadcasted_iota(jnp.int32, arow.shape, 1)
    ) & (arow < pool + qd)
    w = counts[...] * jnp.exp(scores[...] - log_total[0:1]) - jnp.where(positive, 1.0, 0.0)
    weights[...] = w.astype(bf16)
    udot = jnp.sum(
        weights[:pool, :].astype(f32) * scores[:pool, :], axis=1, keepdims=True
    )

    scale_col = nscale[...]
    back = udot * scale_col
    wide = 512

    @pl.loop(0, width // wide)
    def _(b):
        cols = pl.ds(pl.multiple_of(b * wide, wide), wide)
        g = inv_temp * dot_nn(weights[:pool, :], qfull[:, cols])
        gnbuf[:, cols] = (
            scale_col * (g - back * nraw[:, cols].astype(f32))
        ).astype(bf16)

    save = pltpu.make_async_copy(gnbuf, gn_ref, gsem)
    save.start()

    pg = inv_temp * dot_nn(weights[pool : pool + 16, :], qfull[...])
    gp_ref[...] = norm_grad(px, pscale, pg[:qd])

    own16 = jnp.concatenate([own.astype(f32), jnp.zeros((8, nq), f32)], axis=0).astype(bf16)
    own_w = dot_nt(own16, weights[...]).astype(bf16)
    own_g = dot_nn(own_w, unit[...])[:qd]

    u_copy(0, chip).wait_recv()
    acc[...] = sibrecv[chip].astype(f32)

    @pl.loop(1, nc)
    def _(k):
        c_copy(k, behind(k)).wait_recv()
        acc[...] += crecv[k].astype(f32)

    rest = jnp.concatenate([acc[:8, :], acc[8:, :]], axis=1)
    qg = inv_temp * (own_g + rest * jnp.exp(-log_own))
    gq_ref[...] = norm_grad(qx, qscale, qg)

    z_sib.wait_send()
    u_copy(0, chip).wait_send()

    @pl.loop(1, nc)
    def _(k):
        z_copy(k, chip).wait_send()
        u_copy(k, ahead(k)).wait_send()
        c_copy(k, ahead(k)).wait_send()

    for dist in range(outer):
        relay(dist, sent)
        relay_side(dist, sent)

    save.wait()


def local(queries, passages, negatives, pairs):
    n = lax.axis_size("dp")
    nc = n // 2
    qd, width = queries.shape
    pool = negatives.shape[0]
    nq = n * qd
    half = width // 2
    rows = pool + 128
    vm = pl.BlockSpec(memory_space=pltpu.VMEM)
    hbm = pl.BlockSpec(memory_space=pltpu.HBM)
    dma = pltpu.SemaphoreType.DMA
    loss, gq, gp, gn = pl.pallas_call(
        functools.partial(kernel, n),
        out_shape=(
            jax.ShapeDtypeStruct((qd, 1), f32),
            jax.ShapeDtypeStruct((qd, width), f32),
            jax.ShapeDtypeStruct((qd, width), f32),
            jax.ShapeDtypeStruct((pool, width), bf16),
        ),
        in_specs=[hbm, hbm, hbm, hbm],
        out_specs=(vm, vm, vm, hbm),
        scratch_shapes=[
            pltpu.VMEM((qd, width), bf16),
            pltpu.VMEM((qd, width), bf16),
            pltpu.VMEM((2, pairs.shape[0]), jnp.int32),
            pltpu.VMEM((n, 16, half + EXTRA), bf16),
            pltpu.VMEM((nq, width), bf16),
            pltpu.VMEM((pool, width), bf16),
            pltpu.VMEM((rows, width), bf16),
            pltpu.VMEM((pool, 1), f32),
            pltpu.VMEM((rows, nq), f32),
            pltpu.VMEM((rows, nq), f32),
            pltpu.VMEM((nq, rows), bf16),
            pltpu.VMEM((rows, nq), bf16),
            pltpu.VMEM((n, 16, half), bf16),
            pltpu.VMEM((nc, 16, half), bf16),
            pltpu.VMEM((nc, 16, half), bf16),
            pltpu.VMEM((pool, width), bf16),
            pltpu.VMEM((8, nq), f32),
            pltpu.VMEM((8, nq), f32),
            pltpu.VMEM((nc, 8, nq), f32),
            pltpu.VMEM((16, half), f32),
            dma, dma((3,)), dma,
            dma((nc, 2)), dma((nc, inner_size(nc))), dma((nc,)), dma((nc,)), dma((nc,)),
            dma((nc,)), dma((nc,)),
            dma((nc,)), dma((nc,)), dma((1,)), dma((1,)), dma((nc,)), dma((nc,)),
        ],
        compiler_params=pltpu.CompilerParams(
            collective_id=0, has_side_effects=True,
            vmem_limit_bytes=58 * 1024 * 1024,
        ),
    )(queries, passages, negatives, pairs.T)
    return loss.reshape(qd), gq, gp, gn.astype(f32)


def solution(mesh):
    rows = P(("groups", "dp"), None)
    return jax.shard_map(
        local,
        mesh=mesh,
        in_specs=(rows, rows, rows, rows),
        out_specs=(P(("groups", "dp")), rows, rows, rows),
        check_vma=False,
    )
```

```python
import functools

import jax
import jax.numpy as jnp
from jax import lax
from jax.experimental import pallas as pl
from jax.experimental.pallas import tpu as pltpu
from jax.sharding import PartitionSpec as P

inv_temp = 50.0
norm_eps = 1e-06
f32 = jnp.float32
bf16 = jnp.bfloat16
EXTRA = 128


def dot_nt(a, b):
    return lax.dot_general(a, b, (((1,), (1,)), ((), ())), preferred_element_type=f32)


def dot_nn(a, b):
    return lax.dot_general(a, b, (((1,), (0,)), ((), ())), preferred_element_type=f32)


def norm_grad(raw, scale, up):
    dot_sum = jnp.sum(raw * up, axis=1, keepdims=True)
    return scale * up - scale * scale * scale * dot_sum * raw


def inner_size(chips):
    size = 1
    while (2 * size) * (2 * size) <= chips and chips % (2 * size) == 0:
        size *= 2
    return size


def kernel(
    n, q_hbm, p_hbm, neg_ref, pairs_hbm,
    loss_ref, gq_ref, gp_ref, gn_ref,
    q_ref, p_ref, pairs_ref, qbuf, qfull, nraw, unit, nscale, counts, scores, expt, weights, ubuf, sibrecv, crecv, gnbuf,
    zsend, zsib, zbuf, acc,
    nsem, insem, gsem, qs, ys, qr, fs, fr, us, ur, cs, cr, zs, zr, zxs, zxr,
):
    qd, width = q_ref.shape
    half = width // 2
    pool = neg_ref.shape[0]
    npairs = pairs_ref.shape[1]
    nq = n * qd
    nc = n // 2
    inner = inner_size(nc)
    outer = nc // inner
    me = lax.axis_index("dp")
    chip = me // 2
    core = me - 2 * chip
    sib = me + 1 - 2 * core

    a = chip // inner
    b = chip - a * inner

    def ahead(k):
        return lax.rem(chip + k, nc)

    def behind(k):
        return lax.rem(chip + nc - k, nc)

    def remote(src, dst, ssem, rsem, target):
        return pltpu.make_async_remote_copy(
            src_ref=src, dst_ref=dst, send_sem=ssem, recv_sem=rsem,
            device_id={"dp": target}, device_id_type=pl.DeviceIdType.MESH,
        )

    first = pltpu.make_async_copy(q_hbm, q_ref, insem.at[0])
    second = pltpu.make_async_copy(pairs_hbm, pairs_ref, insem.at[1])
    third = pltpu.make_async_copy(p_hbm, p_ref, insem.at[2])
    load = pltpu.make_async_copy(neg_ref, nraw, nsem)
    first.start()
    second.start()
    third.start()
    load.start()
    barrier = pltpu.get_barrier_semaphore()
    pl.semaphore_signal(barrier, inc=1, device_id={"dp": sib}, device_id_type=pl.DeviceIdType.MESH)

    @pl.loop(1, nc)
    def _(k):
        pl.semaphore_signal(
            barrier, inc=1, device_id={"dp": 2 * ahead(k) + core},
            device_id_type=pl.DeviceIdType.MESH,
        )

    first.wait()
    qx = q_ref[...].astype(f32)
    qscale = lax.rsqrt(jnp.sum(qx * qx, axis=1, keepdims=True) + norm_eps)
    qu = qx * qscale
    qbuf[me, :, :half] = jnp.concatenate([qu[:, :half], qu[:, half:]], axis=0).astype(bf16)
    second.wait()
    pv = jnp.concatenate(
        [pairs_ref[...].astype(f32), jnp.full((2, EXTRA - npairs), -1.0, f32)], axis=1
    )
    prow, trow = pv[0:1], pv[1:2]
    owner = jnp.floor((trow + 0.5) * (1.0 / pool))
    local_row = trow - owner * pool
    rid = lax.broadcasted_iota(jnp.int32, (16, EXTRA), 0)
    meta = jnp.where(rid == 0, prow, jnp.where(rid == 1, owner, local_row))
    qbuf[me, :, half:] = meta.astype(bf16)

    pl.semaphore_wait(barrier, nc)

    def along(shift):
        slot = qbuf.at[me]
        target = 2 * (lax.rem(a + shift, outer) * inner + b) + core
        return remote(slot, slot, qs.at[shift], qr.at[chip], target)

    def across(o, shift):
        slot = qbuf.at[2 * o + core]
        target = 2 * (a * inner + lax.rem(b + shift, inner)) + core
        return remote(slot, slot, ys.at[o, shift], qr.at[o], target)

    def hand(o, c):
        slot = qbuf.at[2 * o + c]
        return remote(slot, slot, fs.at[o], fr.at[o], sib)

    def arrived(o):
        slot = qbuf.at[2 * o + core]
        remote(slot, slot, qs.at[0], qr.at[o], sib).wait_recv()

    def line(shift):
        return lax.rem(a + outer - shift, outer)

    def spread(o):
        @pl.loop(1, inner)
        def _(shift):
            across(o, shift).start()

        hand(o, core).start()

    def side(shift, act):
        @pl.loop(1, inner)
        def _(turn):
            act(line(shift) * inner + lax.rem(b + inner - turn, inner))

    def pass_on(o):
        arrived(o)
        hand(o, core).start()

    def passed(o):
        hand(o, core).wait_send()

    for shift in range(1, outer):
        along(shift).start()
    spread(chip)

    third.wait()
    px = p_ref[...].astype(f32)
    pscale = lax.rsqrt(jnp.sum(px * px, axis=1, keepdims=True) + norm_eps)
    unit[pool : pool + 16, :] = jnp.concatenate(
        [px * pscale, jnp.zeros((16 - qd, width), f32)], axis=0
    ).astype(bf16)
    unit[pool + 16 :, :] = jnp.zeros((unit.shape[0] - pool - 16, width), bf16)
    load.wait()

    def normalise(lo, hi):
        @pl.loop(lo, hi)
        def _(blk):
            rows = pl.ds(pl.multiple_of(blk * 16, 16), 16)
            x = nraw[rows, :].astype(f32)
            s = lax.rsqrt(jnp.sum(x * x, axis=1, keepdims=True) + norm_eps)
            nscale[rows, :] = s
            unit[rows, :] = (x * s).astype(bf16)

    blocks = pool // 16
    normalise(0, blocks // outer)
    for shift in range(1, outer):
        o = line(shift) * inner + b
        arrived(o)
        spread(o)
        side(shift - 1, pass_on)
        normalise(blocks * shift // outer, blocks * (shift + 1) // outer)
    side(outer - 1, pass_on)

    arow = lax.broadcasted_iota(jnp.int32, (unit.shape[0], nq), 0)
    counts[...] = jnp.where((arow >= pool) & (arow < pool + qd), 1.0, 0.0)
    mef = me.astype(f32)

    def place(j):
        left = qbuf[2 * j].astype(f32)
        right = qbuf[2 * j + 1].astype(f32)
        rows = pl.ds(pl.multiple_of(j * 16, 16), 16)
        qfull[rows, :half] = jnp.concatenate([left[:8, :half], right[:8, :half]], axis=0).astype(bf16)
        qfull[rows, half:] = jnp.concatenate([left[8:, :half], right[8:, :half]], axis=0).astype(bf16)
        pool_id = lax.broadcasted_iota(jnp.int32, (pool, EXTRA), 0).astype(f32)
        query_id = lax.broadcasted_iota(jnp.int32, (nq, EXTRA), 0).astype(f32)
        hot_t, hot_q = [], []
        for part, c in ((left, 0), (right, 1)):
            m = part[:8, half:]
            want = jnp.where(m[1:2] == mef, m[2:3], -1.0)
            ask = m[0:1] + ((2 * j + c) * qd).astype(f32)
            hot_t.append(jnp.where(pool_id == want, 1.0, 0.0).astype(bf16))
            hot_q.append(jnp.where(query_id == ask, 1.0, 0.0).astype(bf16))
        counts[:pool, :] += dot_nt(
            jnp.concatenate(hot_t, axis=1), jnp.concatenate(hot_q, axis=1)
        )

    hand(chip, 1 - core).wait_recv()
    place(chip)

    @pl.loop(1, nc)
    def _(k):
        hand(behind(k), 1 - core).wait_recv()
        place(behind(k))

    zero = jnp.zeros((1, 128), f32)
    for m in range(nq // 128):
        cols = slice(m * 128, m * 128 + 128)
        s = inv_temp * dot_nt(unit[...], qfull[cols, :])
        scores[:, cols] = s
        e = counts[:, cols] * jnp.exp(s)
        zsend[:, cols] = jnp.broadcast_to(jnp.sum(e, axis=0, keepdims=True) + zero, (8, 128))
        expt[cols, :] = e.T.astype(bf16)

    z_sib = remote(zsend, zsib, zs.at[0], zr.at[0], sib)
    z_sib.start()

    step = 256

    @pl.loop(0, half // step)
    def _(b):
        left = pl.ds(pl.multiple_of(b * step, step), step)
        right = pl.ds(pl.multiple_of(half + b * step, step), step)
        for m in range(nq // 128):
            e = expt[m * 128 : m * 128 + 128, :]
            u0 = dot_nn(e, unit[:, left]).reshape(128 // 8, 8, step)
            u1 = dot_nn(e, unit[:, right]).reshape(128 // 8, 8, step)
            ubuf[m * 16 : m * 16 + 16, :, left] = jnp.concatenate([u0, u1], axis=1).astype(bf16)

    def u_copy(k, j):
        return remote(ubuf.at[2 * j + 1 - core], sibrecv.at[j], us.at[k], ur.at[k], sib)

    @pl.loop(1, nc + 1)
    def _(k):
        u_copy(lax.rem(k, nc), ahead(k)).start()

    z_sib.wait_recv()
    zbuf[chip] = zsend[...] + zsib[...]

    def z_copy(k, slot):
        return remote(zbuf.at[chip], zbuf.at[slot], zxs.at[k], zxr.at[k], 2 * ahead(k) + core)

    @pl.loop(1, nc)
    def _(k):
        z_copy(k, chip).start()

    def c_copy(k, j):
        return remote(
            ubuf.at[2 * j + core], crecv.at[k], cs.at[k], cr.at[k], 2 * j + core
        )

    @pl.loop(1, nc)
    def _(k):
        j = ahead(k)
        u_copy(k, j).wait_recv()
        ubuf[2 * j + core] = (
            ubuf[2 * j + core].astype(f32) + sibrecv[j].astype(f32)
        ).astype(bf16)
        c_copy(k, j).start()

    @pl.loop(1, nc)
    def _(k):
        z_copy(k, behind(k)).wait_recv()

    total = zbuf[0]
    for j in range(1, nc):
        total = total + zbuf[j]
    log_total = jnp.log(total)
    lane_q = lax.broadcasted_iota(jnp.int32, (8, nq), 1)
    row_q = lax.broadcasted_iota(jnp.int32, (8, nq), 0)
    own = lane_q == row_q + me * qd
    log_own = jnp.sum(jnp.where(own, log_total, 0.0), axis=1, keepdims=True)
    self_score = jnp.sum(
        jnp.where(own, scores[pool : pool + 8, :], 0.0), axis=1, keepdims=True
    )
    loss_ref[...] = jnp.sum(
        jnp.where(lane_q == row_q, log_own - self_score, 0.0), axis=0, keepdims=True
    )[:, :128]
    positive = (arow >= pool) & (
        arow - pool + me * qd == lax.broadcasted_iota(jnp.int32, arow.shape, 1)
    ) & (arow < pool + qd)
    w = counts[...] * jnp.exp(scores[...] - log_total[0:1]) - jnp.where(positive, 1.0, 0.0)
    weights[...] = w.astype(bf16)
    udot = jnp.sum(
        weights[:pool, :].astype(f32) * scores[:pool, :], axis=1, keepdims=True
    )

    scale_col = nscale[...]
    back = udot * scale_col
    wide = 512

    @pl.loop(0, width // wide)
    def _(b):
        cols = pl.ds(pl.multiple_of(b * wide, wide), wide)
        g = inv_temp * dot_nn(weights[:pool, :], qfull[:, cols])
        gnbuf[:, cols] = (
            scale_col * (g - back * nraw[:, cols].astype(f32))
        ).astype(bf16)

    save = pltpu.make_async_copy(gnbuf, gn_ref, gsem)
    save.start()

    pg = inv_temp * dot_nn(weights[pool : pool + 16, :], qfull[...])
    gp_ref[...] = norm_grad(px, pscale, pg[:qd])

    own16 = jnp.concatenate([own.astype(f32), jnp.zeros((8, nq), f32)], axis=0).astype(bf16)
    own_w = dot_nt(own16, weights[...]).astype(bf16)
    own_g = dot_nn(own_w, unit[...])[:qd]

    u_copy(0, chip).wait_recv()
    acc[...] = sibrecv[chip].astype(f32)

    @pl.loop(1, nc)
    def _(k):
        c_copy(k, behind(k)).wait_recv()
        acc[...] += crecv[k].astype(f32)

    rest = jnp.concatenate([acc[:8, :], acc[8:, :]], axis=1)
    qg = inv_temp * (own_g + rest * jnp.exp(-log_own))
    gq_ref[...] = norm_grad(qx, qscale, qg)

    z_sib.wait_send()
    u_copy(0, chip).wait_send()

    @pl.loop(1, nc)
    def _(k):
        z_copy(k, chip).wait_send()
        u_copy(k, ahead(k)).wait_send()
        c_copy(k, ahead(k)).wait_send()

    for shift in range(outer):
        if shift:
            along(shift).wait_send()
        o = line(shift) * inner + b
        for turn in range(1, inner):
            across(o, turn).wait_send()
        hand(o, core).wait_send()
        side(shift, passed)

    save.wait()


def finish(loss_ref, gq_ref, gp_ref, gn_ref, loss_out, gq_out, gp_out, gn_out):
    @pl.when(pl.program_id(0) == 0)
    def _():
        loss_out[...] = loss_ref[0, : loss_out.shape[0]]
        gq_out[...] = gq_ref[...]
        gp_out[...] = gp_ref[...]

    gn_out[...] = gn_ref[...].astype(f32)


def local(queries, passages, negatives, pairs):
    n = lax.axis_size("dp")
    nc = n // 2
    qd, width = queries.shape
    pool = negatives.shape[0]
    nq = n * qd
    half = width // 2
    rows = pool + 128
    vm = pl.BlockSpec(memory_space=pltpu.VMEM)
    hbm = pl.BlockSpec(memory_space=pltpu.HBM)
    dma = pltpu.SemaphoreType.DMA
    loss, gq, gp, gn = pl.pallas_call(
        functools.partial(kernel, n),
        out_shape=(
            jax.ShapeDtypeStruct((1, 128), f32),
            jax.ShapeDtypeStruct((qd, width), f32),
            jax.ShapeDtypeStruct((qd, width), f32),
            jax.ShapeDtypeStruct((pool, width), bf16),
        ),
        in_specs=[hbm, hbm, hbm, hbm],
        out_specs=(vm, vm, vm, hbm),
        scratch_shapes=[
            pltpu.VMEM((qd, width), bf16),
            pltpu.VMEM((qd, width), bf16),
            pltpu.VMEM((2, pairs.shape[0]), jnp.int32),
            pltpu.VMEM((n, 16, half + EXTRA), bf16),
            pltpu.VMEM((nq, width), bf16),
            pltpu.VMEM((pool, width), bf16),
            pltpu.VMEM((rows, width), bf16),
            pltpu.VMEM((pool, 1), f32),
            pltpu.VMEM((rows, nq), f32),
            pltpu.VMEM((rows, nq), f32),
            pltpu.VMEM((nq, rows), bf16),
            pltpu.VMEM((rows, nq), bf16),
            pltpu.VMEM((n, 16, half), bf16),
            pltpu.VMEM((nc, 16, half), bf16),
            pltpu.VMEM((nc, 16, half), bf16),
            pltpu.VMEM((pool, width), bf16),
            pltpu.VMEM((8, nq), f32),
            pltpu.VMEM((8, nq), f32),
            pltpu.VMEM((nc, 8, nq), f32),
            pltpu.VMEM((16, half), f32),
            dma, dma((3,)), dma,
            dma((nc // inner_size(nc),)), dma((nc, inner_size(nc))), dma((nc,)), dma((nc,)), dma((nc,)),
            dma((nc,)), dma((nc,)),
            dma((nc,)), dma((nc,)), dma((1,)), dma((1,)), dma((nc,)), dma((nc,)),
        ],
        compiler_params=pltpu.CompilerParams(
            collective_id=0, has_side_effects=True,
            vmem_limit_bytes=58 * 1024 * 1024,
        ),
    )(queries, passages, negatives, pairs.T)
    block = 64
    whole = pl.BlockSpec((qd, width), lambda i: (0, 0))
    piece = pl.BlockSpec((block, width), lambda i: (i, 0))
    return pl.pallas_call(
        finish,
        grid=(pool // block,),
        out_shape=(
            jax.ShapeDtypeStruct((qd,), f32),
            jax.ShapeDtypeStruct((qd, width), f32),
            jax.ShapeDtypeStruct((qd, width), f32),
            jax.ShapeDtypeStruct((pool, width), f32),
        ),
        in_specs=[pl.BlockSpec((1, 128), lambda i: (0, 0)), whole, whole, piece],
        out_specs=(pl.BlockSpec((qd,), lambda i: (0,)), whole, whole, piece),
        compiler_params=pltpu.CompilerParams(vmem_limit_bytes=60 * 1024 * 1024),
    )(loss, gq, gp, gn)


def solution(mesh):
    rows = P(("groups", "dp"), None)
    return jax.shard_map(
        local,
        mesh=mesh,
        in_specs=(rows, rows, rows, rows),
        out_specs=(P(("groups", "dp")), rows, rows, rows),
        check_vma=False,
    )
```

```python
import functools

import jax
import jax.numpy as jnp
from jax import lax
from jax.experimental import pallas as pl
from jax.experimental.pallas import tpu as pltpu
from jax.sharding import PartitionSpec as P

inv_temp = 50.0
norm_eps = 1e-06
f32 = jnp.float32
bf16 = jnp.bfloat16
EXTRA = 128


def dot_nt(a, b):
    return lax.dot_general(a, b, (((1,), (1,)), ((), ())), preferred_element_type=f32)


def dot_nn(a, b):
    return lax.dot_general(a, b, (((1,), (0,)), ((), ())), preferred_element_type=f32)


def norm_grad(raw, scale, up):
    dot_sum = jnp.sum(raw * up, axis=1, keepdims=True)
    return scale * up - scale * scale * scale * dot_sum * raw


def inner_size(chips):
    size = 1
    while (2 * size) * (2 * size) <= chips and chips % (2 * size) == 0:
        size *= 2
    return size


def kernel(
    n, q_hbm, p_hbm, neg_ref, pairs_hbm,
    loss_ref, gq_ref, gp_ref, gn_ref,
    q_ref, p_ref, pairs_ref, qbuf, qfull, nraw, unit, nscale, counts, scores, expt, weights, ubuf, sibrecv, crecv, gnbuf,
    zsend, zsib, zbuf, acc,
    nsem, insem, gsem, qs, ys, qr, fs, fr, us, ur, cs, cr, zs, zr, zxs, zxr,
):
    qd, width = q_ref.shape
    half = width // 2
    pool = neg_ref.shape[0]
    npairs = pairs_ref.shape[1]
    nq = n * qd
    nc = n // 2
    inner = inner_size(nc)
    outer = nc // inner
    me = lax.axis_index("dp")
    chip = me // 2
    core = me - 2 * chip
    sib = me + 1 - 2 * core

    a = chip // inner
    b = chip - a * inner

    def ahead(k):
        return lax.rem(chip + k, nc)

    def behind(k):
        return lax.rem(chip + nc - k, nc)

    def remote(src, dst, ssem, rsem, target):
        return pltpu.make_async_remote_copy(
            src_ref=src, dst_ref=dst, send_sem=ssem, recv_sem=rsem,
            device_id={"dp": target}, device_id_type=pl.DeviceIdType.MESH,
        )

    first = pltpu.make_async_copy(q_hbm, q_ref, insem.at[0])
    second = pltpu.make_async_copy(pairs_hbm, pairs_ref, insem.at[1])
    third = pltpu.make_async_copy(p_hbm, p_ref, insem.at[2])
    load = pltpu.make_async_copy(neg_ref, nraw, nsem)
    first.start()
    second.start()
    third.start()
    load.start()
    barrier = pltpu.get_barrier_semaphore()
    pl.semaphore_signal(barrier, inc=1, device_id={"dp": sib}, device_id_type=pl.DeviceIdType.MESH)

    @pl.loop(1, nc)
    def _(k):
        pl.semaphore_signal(
            barrier, inc=1, device_id={"dp": 2 * ahead(k) + core},
            device_id_type=pl.DeviceIdType.MESH,
        )

    first.wait()
    qx = q_ref[...].astype(f32)
    qscale = lax.rsqrt(jnp.sum(qx * qx, axis=1, keepdims=True) + norm_eps)
    qu = qx * qscale
    qbuf[me, :, :half] = jnp.concatenate([qu[:, :half], qu[:, half:]], axis=0).astype(bf16)
    second.wait()
    pv = jnp.concatenate(
        [pairs_ref[...].astype(f32), jnp.full((2, EXTRA - npairs), -1.0, f32)], axis=1
    )
    prow, trow = pv[0:1], pv[1:2]
    owner = jnp.floor((trow + 0.5) * (1.0 / pool))
    local_row = trow - owner * pool
    rid = lax.broadcasted_iota(jnp.int32, (16, EXTRA), 0)
    meta = jnp.where(rid == 0, prow, jnp.where(rid == 1, owner, local_row))
    qbuf[me, :, half:] = meta.astype(bf16)

    pl.semaphore_wait(barrier, nc)

    def along(shift):
        slot = qbuf.at[me]
        target = 2 * (lax.rem(a + shift, outer) * inner + b) + core
        return remote(slot, slot, qs.at[shift], qr.at[chip], target)

    def across(o, shift):
        slot = qbuf.at[2 * o + core]
        target = 2 * (a * inner + lax.rem(b + shift, inner)) + core
        return remote(slot, slot, ys.at[o, shift], qr.at[o], target)

    def hand(o, c):
        slot = qbuf.at[2 * o + c]
        return remote(slot, slot, fs.at[o], fr.at[o], sib)

    def arrived(o):
        slot = qbuf.at[2 * o + core]
        remote(slot, slot, qs.at[0], qr.at[o], sib).wait_recv()

    def line(shift):
        return lax.rem(a + outer - shift, outer)

    def spread(o):
        @pl.loop(1, inner)
        def _(shift):
            across(o, shift).start()

        hand(o, core).start()

    def side(shift, act):
        @pl.loop(1, inner)
        def _(turn):
            act(line(shift) * inner + lax.rem(b + inner - turn, inner))

    def pass_on(o):
        arrived(o)
        hand(o, core).start()

    def passed(o):
        hand(o, core).wait_send()

    for shift in range(1, outer):
        along(shift).start()
    spread(chip)

    third.wait()
    px = p_ref[...].astype(f32)
    pscale = lax.rsqrt(jnp.sum(px * px, axis=1, keepdims=True) + norm_eps)
    unit[pool : pool + 16, :] = jnp.concatenate(
        [px * pscale, jnp.zeros((16 - qd, width), f32)], axis=0
    ).astype(bf16)
    unit[pool + 16 :, :] = jnp.zeros((unit.shape[0] - pool - 16, width), bf16)
    load.wait()

    def normalise(lo, hi):
        @pl.loop(lo, hi)
        def _(blk):
            rows = pl.ds(pl.multiple_of(blk * 16, 16), 16)
            x = nraw[rows, :].astype(f32)
            s = lax.rsqrt(jnp.sum(x * x, axis=1, keepdims=True) + norm_eps)
            nscale[rows, :] = s
            unit[rows, :] = (x * s).astype(bf16)

    blocks = pool // 16
    normalise(0, blocks // outer)
    for shift in range(1, outer):
        o = line(shift) * inner + b
        arrived(o)
        spread(o)
        side(shift - 1, pass_on)
        normalise(blocks * shift // outer, blocks * (shift + 1) // outer)
    side(outer - 1, pass_on)

    arow = lax.broadcasted_iota(jnp.int32, (unit.shape[0], nq), 0)
    counts[...] = jnp.where((arow >= pool) & (arow < pool + qd), 1.0, 0.0)
    mef = me.astype(f32)

    def place(j):
        left = qbuf[2 * j].astype(f32)
        right = qbuf[2 * j + 1].astype(f32)
        rows = pl.ds(pl.multiple_of(j * 16, 16), 16)
        qfull[rows, :half] = jnp.concatenate([left[:8, :half], right[:8, :half]], axis=0).astype(bf16)
        qfull[rows, half:] = jnp.concatenate([left[8:, :half], right[8:, :half]], axis=0).astype(bf16)
        pool_id = lax.broadcasted_iota(jnp.int32, (pool, EXTRA), 0).astype(f32)
        query_id = lax.broadcasted_iota(jnp.int32, (nq, EXTRA), 0).astype(f32)
        hot_t, hot_q = [], []
        for part, c in ((left, 0), (right, 1)):
            m = part[:8, half:]
            want = jnp.where(m[1:2] == mef, m[2:3], -1.0)
            ask = m[0:1] + ((2 * j + c) * qd).astype(f32)
            hot_t.append(jnp.where(pool_id == want, 1.0, 0.0).astype(bf16))
            hot_q.append(jnp.where(query_id == ask, 1.0, 0.0).astype(bf16))
        counts[:pool, :] += dot_nt(
            jnp.concatenate(hot_t, axis=1), jnp.concatenate(hot_q, axis=1)
        )

    hand(chip, 1 - core).wait_recv()
    place(chip)

    @pl.loop(1, nc)
    def _(k):
        hand(behind(k), 1 - core).wait_recv()
        place(behind(k))

    zero = jnp.zeros((1, 128), f32)
    for m in range(nq // 128):
        cols = slice(m * 128, m * 128 + 128)
        s = inv_temp * dot_nt(unit[...], qfull[cols, :])
        scores[:, cols] = s
        e = counts[:, cols] * jnp.exp(s)
        zsend[:, cols] = jnp.broadcast_to(jnp.sum(e, axis=0, keepdims=True) + zero, (8, 128))
        expt[cols, :] = e.T.astype(bf16)

    z_sib = remote(zsend, zsib, zs.at[0], zr.at[0], sib)
    z_sib.start()

    step = 256

    @pl.loop(0, half // step)
    def _(b):
        left = pl.ds(pl.multiple_of(b * step, step), step)
        right = pl.ds(pl.multiple_of(half + b * step, step), step)
        for m in range(nq // 128):
            e = expt[m * 128 : m * 128 + 128, :]
            u0 = dot_nn(e, unit[:, left]).reshape(128 // 8, 8, step)
            u1 = dot_nn(e, unit[:, right]).reshape(128 // 8, 8, step)
            ubuf[m * 16 : m * 16 + 16, :, left] = jnp.concatenate([u0, u1], axis=1).astype(bf16)

    def u_copy(k, j):
        return remote(ubuf.at[2 * j + 1 - core], sibrecv.at[j], us.at[k], ur.at[k], sib)

    @pl.loop(1, nc + 1)
    def _(k):
        u_copy(lax.rem(k, nc), ahead(k)).start()

    z_sib.wait_recv()
    zbuf[chip] = zsend[...] + zsib[...]

    def z_copy(k, slot):
        return remote(zbuf.at[chip], zbuf.at[slot], zxs.at[k], zxr.at[k], 2 * ahead(k) + core)

    @pl.loop(1, nc)
    def _(k):
        z_copy(k, chip).start()

    def c_copy(k, j):
        return remote(
            ubuf.at[2 * j + core], crecv.at[k], cs.at[k], cr.at[k], 2 * j + core
        )

    @pl.loop(1, nc)
    def _(k):
        j = ahead(k)
        u_copy(k, j).wait_recv()
        ubuf[2 * j + core] = (
            ubuf[2 * j + core].astype(f32) + sibrecv[j].astype(f32)
        ).astype(bf16)
        c_copy(k, j).start()

    @pl.loop(1, nc)
    def _(k):
        z_copy(k, behind(k)).wait_recv()

    total = zbuf[0]
    for j in range(1, nc):
        total = total + zbuf[j]
    log_total = jnp.log(total)
    lane_q = lax.broadcasted_iota(jnp.int32, (8, nq), 1)
    row_q = lax.broadcasted_iota(jnp.int32, (8, nq), 0)
    own = lane_q == row_q + me * qd
    log_own = jnp.sum(jnp.where(own, log_total, 0.0), axis=1, keepdims=True)
    self_score = jnp.sum(
        jnp.where(own, scores[pool : pool + 8, :], 0.0), axis=1, keepdims=True
    )
    loss_ref[...] = jnp.sum(
        jnp.where(lane_q == row_q, log_own - self_score, 0.0), axis=0, keepdims=True
    )[:, :128]
    positive = (arow >= pool) & (
        arow - pool + me * qd == lax.broadcasted_iota(jnp.int32, arow.shape, 1)
    ) & (arow < pool + qd)
    w = counts[...] * jnp.exp(scores[...] - log_total[0:1]) - jnp.where(positive, 1.0, 0.0)
    weights[...] = w.astype(bf16)
    udot = jnp.sum(
        weights[:pool, :].astype(f32) * scores[:pool, :], axis=1, keepdims=True
    )

    scale_col = nscale[...]
    back = udot * scale_col
    wide = 512

    @pl.loop(0, width // wide)
    def _(b):
        cols = pl.ds(pl.multiple_of(b * wide, wide), wide)
        g = inv_temp * dot_nn(weights[:pool, :], qfull[:, cols])
        gnbuf[:, cols] = (
            scale_col * (g - back * nraw[:, cols].astype(f32))
        ).astype(bf16)

    save = pltpu.make_async_copy(gnbuf, gn_ref, gsem)
    save.start()

    pg = inv_temp * dot_nn(weights[pool : pool + 16, :], qfull[...])
    gp_ref[...] = norm_grad(px, pscale, pg[:qd])

    own16 = jnp.concatenate([own.astype(f32), jnp.zeros((8, nq), f32)], axis=0).astype(bf16)
    own_w = dot_nt(own16, weights[...]).astype(bf16)
    own_g = dot_nn(own_w, unit[...])[:qd]

    u_copy(0, chip).wait_recv()
    acc[...] = sibrecv[chip].astype(f32)

    @pl.loop(1, nc)
    def _(k):
        c_copy(k, behind(k)).wait_recv()
        acc[...] += crecv[k].astype(f32)

    rest = jnp.concatenate([acc[:8, :], acc[8:, :]], axis=1)
    qg = inv_temp * (own_g + rest * jnp.exp(-log_own))
    gq_ref[...] = norm_grad(qx, qscale, qg)

    z_sib.wait_send()
    u_copy(0, chip).wait_send()

    @pl.loop(1, nc)
    def _(k):
        z_copy(k, chip).wait_send()
        u_copy(k, ahead(k)).wait_send()
        c_copy(k, ahead(k)).wait_send()

    for shift in range(outer):
        if shift:
            along(shift).wait_send()
        o = line(shift) * inner + b
        for turn in range(1, inner):
            across(o, turn).wait_send()
        hand(o, core).wait_send()
        side(shift, passed)

    save.wait()


def finish(
    loss_ref, gq_ref, gp_ref, gn_ref, loss_out, gq_out, gp_out, gn_out,
    narrow, full, in_sem, out_sem, q_sem, p_sem,
):
    parts = 8
    block = narrow.shape[0] // parts
    rows = [pl.ds(i * block, block) for i in range(parts)]
    reads = [
        pltpu.make_async_copy(gn_ref.at[r], narrow.at[r], in_sem.at[i])
        for i, r in enumerate(rows)
    ]
    writes = [
        pltpu.make_async_copy(full.at[r], gn_out.at[r], out_sem.at[i])
        for i, r in enumerate(rows)
    ]
    q_copy = pltpu.make_async_copy(gq_ref, gq_out, q_sem)
    p_copy = pltpu.make_async_copy(gp_ref, gp_out, p_sem)
    for read in reads:
        read.start()
    q_copy.start()
    p_copy.start()
    loss_out[...] = loss_ref[0, : loss_out.shape[0]]
    for i, r in enumerate(rows):
        reads[i].wait()
        full[r, :] = narrow[r, :].astype(f32)
        writes[i].start()
    for write in writes:
        write.wait()
    q_copy.wait()
    p_copy.wait()


def local(queries, passages, negatives, pairs):
    n = lax.axis_size("dp")
    nc = n // 2
    qd, width = queries.shape
    pool = negatives.shape[0]
    nq = n * qd
    half = width // 2
    rows = pool + 128
    vm = pl.BlockSpec(memory_space=pltpu.VMEM)
    hbm = pl.BlockSpec(memory_space=pltpu.HBM)
    dma = pltpu.SemaphoreType.DMA
    loss, gq, gp, gn = pl.pallas_call(
        functools.partial(kernel, n),
        out_shape=(
            jax.ShapeDtypeStruct((1, 128), f32),
            jax.ShapeDtypeStruct((qd, width), f32),
            jax.ShapeDtypeStruct((qd, width), f32),
            jax.ShapeDtypeStruct((pool, width), bf16),
        ),
        in_specs=[hbm, hbm, hbm, hbm],
        out_specs=(vm, vm, vm, hbm),
        scratch_shapes=[
            pltpu.VMEM((qd, width), bf16),
            pltpu.VMEM((qd, width), bf16),
            pltpu.VMEM((2, pairs.shape[0]), jnp.int32),
            pltpu.VMEM((n, 16, half + EXTRA), bf16),
            pltpu.VMEM((nq, width), bf16),
            pltpu.VMEM((pool, width), bf16),
            pltpu.VMEM((rows, width), bf16),
            pltpu.VMEM((pool, 1), f32),
            pltpu.VMEM((rows, nq), f32),
            pltpu.VMEM((rows, nq), f32),
            pltpu.VMEM((nq, rows), bf16),
            pltpu.VMEM((rows, nq), bf16),
            pltpu.VMEM((n, 16, half), bf16),
            pltpu.VMEM((nc, 16, half), bf16),
            pltpu.VMEM((nc, 16, half), bf16),
            pltpu.VMEM((pool, width), bf16),
            pltpu.VMEM((8, nq), f32),
            pltpu.VMEM((8, nq), f32),
            pltpu.VMEM((nc, 8, nq), f32),
            pltpu.VMEM((16, half), f32),
            dma, dma((3,)), dma,
            dma((nc // inner_size(nc),)), dma((nc, inner_size(nc))), dma((nc,)), dma((nc,)), dma((nc,)),
            dma((nc,)), dma((nc,)),
            dma((nc,)), dma((nc,)), dma((1,)), dma((1,)), dma((nc,)), dma((nc,)),
        ],
        compiler_params=pltpu.CompilerParams(
            collective_id=0, has_side_effects=True,
            vmem_limit_bytes=58 * 1024 * 1024,
        ),
    )(queries, passages, negatives, pairs.T)
    return pl.pallas_call(
        finish,
        out_shape=(
            jax.ShapeDtypeStruct((qd,), f32),
            jax.ShapeDtypeStruct((qd, width), f32),
            jax.ShapeDtypeStruct((qd, width), f32),
            jax.ShapeDtypeStruct((pool, width), f32),
        ),
        in_specs=[vm, hbm, hbm, hbm],
        out_specs=(vm, hbm, hbm, hbm),
        scratch_shapes=[
            pltpu.VMEM((pool, width), bf16), pltpu.VMEM((pool, width), f32),
            dma((8,)), dma((8,)), dma, dma,
        ],
        compiler_params=pltpu.CompilerParams(vmem_limit_bytes=60 * 1024 * 1024),
    )(loss, gq, gp, gn)


def solution(mesh):
    rows = P(("groups", "dp"), None)
    return jax.shard_map(
        local,
        mesh=mesh,
        in_specs=(rows, rows, rows, rows),
        out_specs=(P(("groups", "dp")), rows, rows, rows),
        check_vma=False,
    )
```

```python
import functools

import jax
import jax.numpy as jnp
from jax import lax
from jax.experimental import pallas as pl
from jax.experimental.pallas import tpu as pltpu
from jax.sharding import PartitionSpec as P

inv_temp = 50.0
norm_eps = 1e-06
f32 = jnp.float32
bf16 = jnp.bfloat16
EXTRA = 128


def dot_nt(a, b):
    return lax.dot_general(a, b, (((1,), (1,)), ((), ())), preferred_element_type=f32)


def dot_nn(a, b):
    return lax.dot_general(a, b, (((1,), (0,)), ((), ())), preferred_element_type=f32)


def norm_grad(raw, scale, up):
    dot_sum = jnp.sum(raw * up, axis=1, keepdims=True)
    return scale * up - scale * scale * scale * dot_sum * raw


def inner_size(chips):
    size = 1
    while (2 * size) * (2 * size) <= chips and chips % (2 * size) == 0:
        size *= 2
    return size


def kernel(
    n, q_hbm, p_hbm, neg_ref, pairs_hbm,
    loss_ref, gq_ref, gp_ref, gn_ref,
    q_ref, p_ref, pairs_ref, qbuf, qfull, nraw, unit, nscale, counts, scores, expt, weights, ubuf, sibrecv, crecv, gnbuf,
    zsend, zsib, zbuf, acc,
    nsem, insem, gsem, qs, ys, qr, fs, fr, us, ur, cs, cr, zs, zr, zxs, zxr,
):
    qd, width = q_ref.shape
    half = width // 2
    pool = neg_ref.shape[0]
    npairs = pairs_ref.shape[1]
    nq = n * qd
    nc = n // 2
    inner = inner_size(nc)
    outer = nc // inner
    me = lax.axis_index("dp")
    chip = me // 2
    core = me - 2 * chip
    sib = me + 1 - 2 * core

    a = chip // inner
    b = chip - a * inner

    def ahead(k):
        return lax.rem(chip + k, nc)

    def behind(k):
        return lax.rem(chip + nc - k, nc)

    def remote(src, dst, ssem, rsem, target):
        return pltpu.make_async_remote_copy(
            src_ref=src, dst_ref=dst, send_sem=ssem, recv_sem=rsem,
            device_id={"dp": target}, device_id_type=pl.DeviceIdType.MESH,
        )

    first = pltpu.make_async_copy(q_hbm, q_ref, insem.at[0])
    second = pltpu.make_async_copy(pairs_hbm, pairs_ref, insem.at[1])
    third = pltpu.make_async_copy(p_hbm, p_ref, insem.at[2])
    load = pltpu.make_async_copy(neg_ref, nraw, nsem)
    first.start()
    second.start()
    third.start()
    load.start()
    barrier = pltpu.get_barrier_semaphore()
    pl.semaphore_signal(barrier, inc=1, device_id={"dp": sib}, device_id_type=pl.DeviceIdType.MESH)

    @pl.loop(1, nc)
    def _(k):
        pl.semaphore_signal(
            barrier, inc=1, device_id={"dp": 2 * ahead(k) + core},
            device_id_type=pl.DeviceIdType.MESH,
        )

    first.wait()
    qx = q_ref[...].astype(f32)
    qscale = lax.rsqrt(jnp.sum(qx * qx, axis=1, keepdims=True) + norm_eps)
    qu = qx * qscale
    qbuf[me, :, :half] = jnp.concatenate([qu[:, :half], qu[:, half:]], axis=0).astype(bf16)
    second.wait()
    pv = jnp.concatenate(
        [pairs_ref[...].astype(f32), jnp.full((2, EXTRA - npairs), -1.0, f32)], axis=1
    )
    prow, trow = pv[0:1], pv[1:2]
    owner = jnp.floor((trow + 0.5) * (1.0 / pool))
    local_row = trow - owner * pool
    rid = lax.broadcasted_iota(jnp.int32, (16, EXTRA), 0)
    meta = jnp.where(rid == 0, prow, jnp.where(rid == 1, owner, local_row))
    qbuf[me, :, half:] = meta.astype(bf16)

    pl.semaphore_wait(barrier, nc)

    def along(shift):
        slot = qbuf.at[me]
        target = 2 * (lax.rem(a + shift, outer) * inner + b) + core
        return remote(slot, slot, qs.at[shift], qr.at[chip], target)

    def across(o, shift):
        slot = qbuf.at[2 * o + core]
        target = 2 * (a * inner + lax.rem(b + shift, inner)) + core
        return remote(slot, slot, ys.at[o, shift], qr.at[o], target)

    def hand(o, c):
        slot = qbuf.at[2 * o + c]
        return remote(slot, slot, fs.at[o], fr.at[o], sib)

    def arrived(o):
        slot = qbuf.at[2 * o + core]
        remote(slot, slot, qs.at[0], qr.at[o], sib).wait_recv()

    def line(shift):
        return lax.rem(a + outer - shift, outer)

    def spread(o):
        @pl.loop(1, inner)
        def _(shift):
            across(o, shift).start()

        hand(o, core).start()

    def side(shift, act):
        @pl.loop(1, inner)
        def _(turn):
            act(line(shift) * inner + lax.rem(b + inner - turn, inner))

    def pass_on(o):
        arrived(o)
        hand(o, core).start()

    def passed(o):
        hand(o, core).wait_send()

    for shift in range(1, outer):
        along(shift).start()
    spread(chip)

    third.wait()
    px = p_ref[...].astype(f32)
    pscale = lax.rsqrt(jnp.sum(px * px, axis=1, keepdims=True) + norm_eps)
    unit[pool : pool + 16, :] = jnp.concatenate(
        [px * pscale, jnp.zeros((16 - qd, width), f32)], axis=0
    ).astype(bf16)
    unit[pool + 16 :, :] = jnp.zeros((unit.shape[0] - pool - 16, width), bf16)
    load.wait()

    def normalise(lo, hi):
        @pl.loop(lo, hi)
        def _(blk):
            rows = pl.ds(pl.multiple_of(blk * 16, 16), 16)
            x = nraw[rows, :].astype(f32)
            s = lax.rsqrt(jnp.sum(x * x, axis=1, keepdims=True) + norm_eps)
            nscale[rows, :] = s
            unit[rows, :] = (x * s).astype(bf16)

    blocks = pool // 16
    normalise(0, blocks // outer)
    for shift in range(1, outer):
        o = line(shift) * inner + b
        arrived(o)
        spread(o)
        side(shift - 1, pass_on)
        normalise(blocks * shift // outer, blocks * (shift + 1) // outer)
    side(outer - 1, pass_on)

    arow = lax.broadcasted_iota(jnp.int32, (unit.shape[0], nq), 0)
    counts[...] = jnp.where((arow >= pool) & (arow < pool + qd), 1.0, 0.0)
    mef = me.astype(f32)

    def place(j):
        left = qbuf[2 * j].astype(f32)
        right = qbuf[2 * j + 1].astype(f32)
        rows = pl.ds(pl.multiple_of(j * 16, 16), 16)
        qfull[rows, :half] = jnp.concatenate([left[:8, :half], right[:8, :half]], axis=0).astype(bf16)
        qfull[rows, half:] = jnp.concatenate([left[8:, :half], right[8:, :half]], axis=0).astype(bf16)
        pool_id = lax.broadcasted_iota(jnp.int32, (pool, EXTRA), 0).astype(f32)
        query_id = lax.broadcasted_iota(jnp.int32, (nq, EXTRA), 0).astype(f32)
        hot_t, hot_q = [], []
        for part, c in ((left, 0), (right, 1)):
            m = part[:8, half:]
            want = jnp.where(m[1:2] == mef, m[2:3], -1.0)
            ask = m[0:1] + ((2 * j + c) * qd).astype(f32)
            hot_t.append(jnp.where(pool_id == want, 1.0, 0.0).astype(bf16))
            hot_q.append(jnp.where(query_id == ask, 1.0, 0.0).astype(bf16))
        counts[:pool, :] += dot_nt(
            jnp.concatenate(hot_t, axis=1), jnp.concatenate(hot_q, axis=1)
        )

    hand(chip, 1 - core).wait_recv()
    place(chip)

    @pl.loop(1, nc)
    def _(k):
        hand(behind(k), 1 - core).wait_recv()
        place(behind(k))

    zero = jnp.zeros((1, 128), f32)
    for m in range(nq // 128):
        cols = slice(m * 128, m * 128 + 128)
        s = inv_temp * dot_nt(unit[...], qfull[cols, :])
        scores[:, cols] = s
        e = counts[:, cols] * jnp.exp(s)
        zsend[:, cols] = jnp.broadcast_to(jnp.sum(e, axis=0, keepdims=True) + zero, (8, 128))
        expt[cols, :] = e.T.astype(bf16)

    z_sib = remote(zsend, zsib, zs.at[0], zr.at[0], sib)
    z_sib.start()

    step = 256

    @pl.loop(0, half // step)
    def _(b):
        left = pl.ds(pl.multiple_of(b * step, step), step)
        right = pl.ds(pl.multiple_of(half + b * step, step), step)
        for m in range(nq // 128):
            e = expt[m * 128 : m * 128 + 128, :]
            u0 = dot_nn(e, unit[:, left]).reshape(128 // 8, 8, step)
            u1 = dot_nn(e, unit[:, right]).reshape(128 // 8, 8, step)
            ubuf[m * 16 : m * 16 + 16, :, left] = jnp.concatenate([u0, u1], axis=1).astype(bf16)

    def u_copy(k, j):
        return remote(ubuf.at[2 * j + 1 - core], sibrecv.at[j], us.at[k], ur.at[k], sib)

    @pl.loop(1, nc + 1)
    def _(k):
        u_copy(lax.rem(k, nc), ahead(k)).start()

    z_sib.wait_recv()
    zbuf[chip] = zsend[...] + zsib[...]

    def z_copy(k, slot):
        return remote(zbuf.at[chip], zbuf.at[slot], zxs.at[k], zxr.at[k], 2 * ahead(k) + core)

    @pl.loop(1, nc)
    def _(k):
        z_copy(k, chip).start()

    def c_copy(k, j):
        return remote(
            ubuf.at[2 * j + core], crecv.at[k], cs.at[k], cr.at[k], 2 * j + core
        )

    @pl.loop(1, nc)
    def _(k):
        j = ahead(k)
        u_copy(k, j).wait_recv()
        ubuf[2 * j + core] = (
            ubuf[2 * j + core].astype(f32) + sibrecv[j].astype(f32)
        ).astype(bf16)
        c_copy(k, j).start()

    @pl.loop(1, nc)
    def _(k):
        z_copy(k, behind(k)).wait_recv()

    total = zbuf[0]
    for j in range(1, nc):
        total = total + zbuf[j]
    log_total = jnp.log(total)
    lane_q = lax.broadcasted_iota(jnp.int32, (8, nq), 1)
    row_q = lax.broadcasted_iota(jnp.int32, (8, nq), 0)
    own = lane_q == row_q + me * qd
    log_own = jnp.sum(jnp.where(own, log_total, 0.0), axis=1, keepdims=True)
    self_score = jnp.sum(
        jnp.where(own, scores[pool : pool + 8, :], 0.0), axis=1, keepdims=True
    )
    loss_ref[...] = jnp.sum(
        jnp.where(lane_q == row_q, log_own - self_score, 0.0), axis=0, keepdims=True
    )[:, :128]
    positive = (arow >= pool) & (
        arow - pool + me * qd == lax.broadcasted_iota(jnp.int32, arow.shape, 1)
    ) & (arow < pool + qd)
    w = counts[...] * jnp.exp(scores[...] - log_total[0:1]) - jnp.where(positive, 1.0, 0.0)
    weights[...] = w.astype(bf16)
    udot = jnp.sum(
        weights[:pool, :].astype(f32) * scores[:pool, :], axis=1, keepdims=True
    )

    scale_col = nscale[...]
    back = udot * scale_col
    wide = 512

    @pl.loop(0, width // wide)
    def _(b):
        cols = pl.ds(pl.multiple_of(b * wide, wide), wide)
        g = inv_temp * dot_nn(weights[:pool, :], qfull[:, cols])
        gnbuf[:, cols] = (
            scale_col * (g - back * nraw[:, cols].astype(f32))
        ).astype(bf16)

    save = pltpu.make_async_copy(gnbuf, gn_ref, gsem)
    save.start()

    pg = inv_temp * dot_nn(weights[pool : pool + 16, :], qfull[...])
    gp_ref[...] = norm_grad(px, pscale, pg[:qd])

    own16 = jnp.concatenate([own.astype(f32), jnp.zeros((8, nq), f32)], axis=0).astype(bf16)
    own_w = dot_nt(own16, weights[...]).astype(bf16)
    own_g = dot_nn(own_w, unit[...])[:qd]

    u_copy(0, chip).wait_recv()
    acc[...] = sibrecv[chip].astype(f32)

    @pl.loop(1, nc)
    def _(k):
        c_copy(k, behind(k)).wait_recv()
        acc[...] += crecv[k].astype(f32)

    rest = jnp.concatenate([acc[:8, :], acc[8:, :]], axis=1)
    qg = inv_temp * (own_g + rest * jnp.exp(-log_own))
    gq_ref[...] = norm_grad(qx, qscale, qg)

    z_sib.wait_send()
    u_copy(0, chip).wait_send()

    @pl.loop(1, nc)
    def _(k):
        z_copy(k, chip).wait_send()
        u_copy(k, ahead(k)).wait_send()
        c_copy(k, ahead(k)).wait_send()

    for shift in range(outer):
        if shift:
            along(shift).wait_send()
        o = line(shift) * inner + b
        for turn in range(1, inner):
            across(o, turn).wait_send()
        hand(o, core).wait_send()
        side(shift, passed)

    save.wait()


def finish(
    loss_ref, gq_ref, gp_ref, gn_ref, loss_out, gq_out, gp_out, gn_out,
    narrow, full, in_sem, out_sem,
):
    parts = 8
    block = narrow.shape[0] // parts
    rows = [pl.ds(i * block, block) for i in range(parts)]
    reads = [
        pltpu.make_async_copy(gn_ref.at[r], narrow.at[r], in_sem.at[i])
        for i, r in enumerate(rows)
    ]
    writes = [
        pltpu.make_async_copy(full.at[r], gn_out.at[r], out_sem.at[i])
        for i, r in enumerate(rows)
    ]
    for read in reads:
        read.start()
    gq_out[...] = gq_ref[...]
    gp_out[...] = gp_ref[...]
    loss_out[...] = loss_ref[0, : loss_out.shape[0]]
    for i, r in enumerate(rows):
        reads[i].wait()
        full[r, :] = narrow[r, :].astype(f32)
        writes[i].start()
    for write in writes:
        write.wait()


def local(queries, passages, negatives, pairs):
    n = lax.axis_size("dp")
    nc = n // 2
    qd, width = queries.shape
    pool = negatives.shape[0]
    nq = n * qd
    half = width // 2
    rows = pool + 128
    vm = pl.BlockSpec(memory_space=pltpu.VMEM)
    hbm = pl.BlockSpec(memory_space=pltpu.HBM)
    dma = pltpu.SemaphoreType.DMA
    loss, gq, gp, gn = pl.pallas_call(
        functools.partial(kernel, n),
        out_shape=(
            jax.ShapeDtypeStruct((1, 128), f32),
            jax.ShapeDtypeStruct((qd, width), f32),
            jax.ShapeDtypeStruct((qd, width), f32),
            jax.ShapeDtypeStruct((pool, width), bf16),
        ),
        in_specs=[hbm, hbm, hbm, hbm],
        out_specs=(vm, vm, vm, hbm),
        scratch_shapes=[
            pltpu.VMEM((qd, width), bf16),
            pltpu.VMEM((qd, width), bf16),
            pltpu.VMEM((2, pairs.shape[0]), jnp.int32),
            pltpu.VMEM((n, 16, half + EXTRA), bf16),
            pltpu.VMEM((nq, width), bf16),
            pltpu.VMEM((pool, width), bf16),
            pltpu.VMEM((rows, width), bf16),
            pltpu.VMEM((pool, 1), f32),
            pltpu.VMEM((rows, nq), f32),
            pltpu.VMEM((rows, nq), f32),
            pltpu.VMEM((nq, rows), bf16),
            pltpu.VMEM((rows, nq), bf16),
            pltpu.VMEM((n, 16, half), bf16),
            pltpu.VMEM((nc, 16, half), bf16),
            pltpu.VMEM((nc, 16, half), bf16),
            pltpu.VMEM((pool, width), bf16),
            pltpu.VMEM((8, nq), f32),
            pltpu.VMEM((8, nq), f32),
            pltpu.VMEM((nc, 8, nq), f32),
            pltpu.VMEM((16, half), f32),
            dma, dma((3,)), dma,
            dma((nc // inner_size(nc),)), dma((nc, inner_size(nc))), dma((nc,)), dma((nc,)), dma((nc,)),
            dma((nc,)), dma((nc,)),
            dma((nc,)), dma((nc,)), dma((1,)), dma((1,)), dma((nc,)), dma((nc,)),
        ],
        compiler_params=pltpu.CompilerParams(
            collective_id=0, has_side_effects=True,
            vmem_limit_bytes=58 * 1024 * 1024,
        ),
    )(queries, passages, negatives, pairs.T)
    return pl.pallas_call(
        finish,
        out_shape=(
            jax.ShapeDtypeStruct((qd,), f32),
            jax.ShapeDtypeStruct((qd, width), f32),
            jax.ShapeDtypeStruct((qd, width), f32),
            jax.ShapeDtypeStruct((pool, width), f32),
        ),
        in_specs=[vm, vm, vm, hbm],
        out_specs=(vm, vm, vm, hbm),
        scratch_shapes=[
            pltpu.VMEM((pool, width), bf16), pltpu.VMEM((pool, width), f32),
            dma((8,)), dma((8,)),
        ],
        compiler_params=pltpu.CompilerParams(vmem_limit_bytes=60 * 1024 * 1024),
    )(loss, gq, gp, gn)


def solution(mesh):
    rows = P(("groups", "dp"), None)
    return jax.shard_map(
        local,
        mesh=mesh,
        in_specs=(rows, rows, rows, rows),
        out_specs=(P(("groups", "dp")), rows, rows, rows),
        check_vma=False,
    )
```
